256 devices in a mesh: tok: 8 (over x, y_lo), feat: 32 (over z, y_hi, core).
Axes of the slice: x: 4, y: 4 (y_hi: 2, y_lo: 2; y = y_hi * 2 + y_lo), z: 8, core: 2. Of those that a mesh axis runs over, the one named last changes fastest.
Arguments:
- query_acts: bfloat16 [2, 384, 8192], P(None, None, 'feat'), may hold values from -6 to 6
- query_grads: bfloat16 [2, 384, 28672], P(None, 'feat', 'tok'), may hold values from -6 to 6
- train_acts: bfloat16 [128, 8192], P(None, 'feat'), may hold values from -6 to 6
- basis_in: bfloat16 [8192, 8192], P('feat', 'tok'), may hold values from -0.0625 to 0.0625
- basis_out: bfloat16 [28672, 28672], P('tok', 'feat'), may hold values from -0.0625 to 0.0625
- eigen_grid: float32 [28672, 8192], P('feat', 'tok'), may hold values from 0.5 to 8
Outputs:
- pulled: bfloat16 [28672, 2, 128], P(('tok', 'feat'))
The draws below stay inside these ranges and needn't reach their ends.
All inputs are finite; a program needn't handle non-finite values.
Results may differ from the reference program's by a relative error of at most 0.0057.
Values may be sent and summed in bfloat16 or wider, within the bound.
No kernel may reach another device: no remote copies, remote signals or barrier semaphores. Data moves between devices by JAX's collectives and lax.ppermute only.
A program may use at most 64 MiB of HBM per device.

```python
import math
import jax
import jax.numpy as jnp
from jax import lax

D = 8192
FF = 28672
QUERIES = 2
QTOK = 384
KTRAIN = 128


def with_spikes(array, own_key, source, target, shards_of, factor):
    owner, partner = [(jnp.arange(array.shape[axis_at]) // (array.shape[axis_at] // shards_of)).reshape([-1 if axis == axis_at else 1 for axis in range(array.ndim)]) for axis_at in (source, target)]
    chosen = jax.random.permutation(own_key, shards_of)[partner]
    strong = (owner == chosen) | (owner == (partner + shards_of // 2) % shards_of)
    return jnp.where(strong, factor * array, array)


def steps_of(key, extent, shards, least, high):
    gain = 1.0
    for position, blocks in shards:
        draws = jax.random.uniform(jax.random.fold_in(jax.random.fold_in(key, 6), position), (blocks,), jnp.float32, least / len(shards), high / len(shards))
        gain = gain * jnp.repeat(jnp.exp(draws), extent[position] // blocks).reshape((-1,) + (1,) * (len(extent) - 1 - position))
    return gain


def scatter_about(own_key, shape, spread, limit, shards=(), held_as=jnp.bfloat16):
    factor_of = steps_of(own_key, shape, shards, -0.22, 0.18) if shards else 1.0
    result = jax.random.normal(own_key, shape, jnp.float32) * spread * factor_of
    return jnp.minimum(jnp.maximum(result, -limit), limit).astype(held_as)


def bell_draw_with(own_key, extent, width, limit, pieces, heavy, kind=jnp.bfloat16):
    result = width * jax.random.normal(own_key, extent, jnp.float32)
    if pieces:
        result = result * steps_of(own_key, extent, pieces, -0.22, 0.18)
    return jnp.clip(with_spikes(result, jax.random.fold_in(own_key, 3), *heavy), -limit, limit).astype(kind)


def setup_inputs(seed: int = 0) -> dict:
    seeds = jax.random.split(jax.random.key(seed), 7)
    return {
        "query_acts": scatter_about(seeds[0], (QUERIES, QTOK, D), 1.0, 6.0, ((2, 32),)),
        "query_grads": scatter_about(seeds[1], (QUERIES, QTOK, FF), 1.0, 6.0, ((1, 32), (2, 8))),
        "train_acts": scatter_about(seeds[2], (KTRAIN, D), 1.0, 6.0, ((1, 32),)),
        "basis_in": scatter_about(seeds[3], (D, D), D ** -0.5, 0.0625, ((0, 32), (1, 8))),
        "basis_out": bell_draw_with(seeds[4], (FF, FF), FF ** -0.5, 0.0625, ((0, 8), (1, 32)), (1, 0, 32, 2.75)),
        "eigen_grid": jnp.clip(jnp.exp(math.log(8.0) - 2.7725887 * jax.random.uniform(seeds[5], (FF, D), jnp.float32) ** steps_of(seeds[5], (FF, D), ((0, 32), (1, 8)), -0.2, 0.2)), 0.5, 8.0),
    }


def reference(query_acts, query_grads, train_acts, basis_in, basis_out, eigen_grid):
    basis_float = basis_in.astype(jnp.float32)
    act_flat = query_acts.reshape(QUERIES * QTOK, D).astype(jnp.float32)
    act_eigen = jnp.dot(act_flat, basis_float, preferred_element_type=jnp.float32).astype(jnp.bfloat16)
    act_float = act_eigen.reshape(QUERIES, QTOK, D).astype(jnp.float32)
    train_eigen = jnp.dot(train_acts.astype(jnp.float32), basis_float, preferred_element_type=jnp.float32).astype(jnp.bfloat16)
    train_float = train_eigen.astype(jnp.float32)
    grad_flat = query_grads.reshape(QUERIES * QTOK, FF).astype(jnp.float32)
    block_count = 8
    block_width = FF // block_count
    block_ids = jnp.arange(block_count, dtype=jnp.int32)

    def one_block(block_index):
        first_col = block_index * block_width
        columns = lax.dynamic_slice_in_dim(basis_out, first_col, block_width, 1).astype(jnp.float32)
        grad_eigen = jnp.dot(grad_flat, columns, preferred_element_type=jnp.float32).astype(jnp.bfloat16)
        grad_float = grad_eigen.reshape(QUERIES, QTOK, block_width).astype(jnp.float32)
        gram_block = jnp.einsum('qte,qtd->qed', grad_float, act_float)
        grid_block = lax.dynamic_slice_in_dim(eigen_grid, first_col, block_width, 0)
        precond = gram_block * (1.0 / QTOK) / grid_block
        probe_block = jnp.einsum('qed,kd->eqk', precond, train_float, precision=lax.Precision.HIGHEST)
        return probe_block

    probe_eigen = lax.map(one_block, block_ids).reshape(FF, QUERIES * KTRAIN)

    def out_block(block_index):
        rows_block = lax.dynamic_slice_in_dim(basis_out, block_index * block_width, block_width, 0).astype(jnp.float32)
        return jnp.dot(rows_block, probe_eigen, preferred_element_type=jnp.float32, precision=lax.Precision.HIGHEST).astype(jnp.bfloat16)

    pulled = lax.map(out_block, block_ids).reshape(FF, QUERIES, KTRAIN)
    return pulled
```

```python
import jax
import jax.numpy as jnp
from jax import lax
from jax.sharding import Mesh, PartitionSpec as P

BF16 = jnp.bfloat16
F32 = jnp.float32
SIZES = {"x": 4, "ylo": 2, "z": 8, "yhi": 2, "core": 2}
TOK = ("x", "ylo")
FEAT = ("z", "yhi", "core")


def shift(array, axis, by):
    size = SIZES[axis]
    return lax.ppermute(array, axis, [(i, (i + by) % size) for i in range(size)])


def ring_of_eight(own, half):
    forward = backward = own
    blocks = [own] + [None] * 7
    for hop in (1, 2, 3):
        forward, backward = shift(forward, "z", 1), shift(backward, "z", -1)
        blocks[8 - hop], blocks[hop] = forward, backward
    far = [shift(forward[:half], "z", 1), shift(backward[half:], "z", -1)]
    blocks[4] = jnp.concatenate(far, axis=0)
    return blocks


def ring_of_four(own, half):
    forward, backward = shift(own, "x", 1), shift(own, "x", -1)
    far = [shift(forward[:half], "x", 1), shift(backward[half:], "x", -1)]
    return [own, backward, jnp.concatenate(far, axis=0), forward]


def tok_offset(by_x, by_y):
    return [
        (x * 2 + y, (x + by_x) % 4 * 2 + (y + by_y) % 2)
        for x in range(4)
        for y in range(2)
    ]


def scatter_tok(pieces, x, ylo):
    total = None
    arrived = []
    for by_x, by_y in ((2, 1), (2, 0), (1, 1), (3, 1), (1, 0), (3, 0), (0, 1)):
        target = (x + by_x) % 4 * 2 + (ylo + by_y) % 2
        piece = lax.dynamic_index_in_dim(pieces, target, 0, keepdims=False)
        arrived.append(lax.ppermute(piece.astype(BF16), TOK, tok_offset(by_x, by_y)))
    total = lax.dynamic_index_in_dim(pieces, x * 2 + ylo, 0, keepdims=False)
    for part in arrived:
        total = total + part.astype(F32)
    return total


def gather_tok(own):
    half = own.shape[0] // 32 * 16
    other = shift(own, "ylo", 1)
    return [ring_of_four(own, half), ring_of_four(other, half)]


def roll_blocks(array, by, axis):
    size = array.shape[axis]
    twice = jnp.concatenate([array, array], axis=axis)
    return lax.dynamic_slice_in_dim(twice, by, size, axis)


def per_device(query_acts, query_grads, train_acts, basis_in, basis_out, eigen_grid):
    x, ylo, z, yhi, core = (lax.axis_index(a) for a in ("x", "ylo", "z", "yhi", "core"))

    own = query_grads.reshape(24, 3584)
    planes = [ring_of_eight(own, 8), ring_of_eight(shift(own, "yhi", 1), 8)]
    half_grads = jnp.concatenate([b for plane in planes for b in plane], axis=0)
    other_grads = shift(half_grads, "core", 1)

    acts = jnp.concatenate([query_acts.reshape(768, 256), train_acts], axis=0)
    partial = jnp.dot(acts, basis_in, preferred_element_type=F32)
    by_core = partial.reshape(2, 448, 2, 512)
    keep = lax.dynamic_index_in_dim(by_core, core, 0, keepdims=False)
    give = lax.dynamic_index_in_dim(by_core, 1 - core, 0, keepdims=False)
    chip_sum = keep + shift(give, "core", 1)
    keep = lax.dynamic_index_in_dim(chip_sum, yhi, 1, keepdims=False)
    give = lax.dynamic_index_in_dim(chip_sum, 1 - yhi, 1, keepdims=False)
    pair_sum = keep + shift(give.astype(BF16), "yhi", 1).astype(F32)
    rows = pair_sum.reshape(8, 56, 512)
    total = lax.dynamic_index_in_dim(rows, z, 0, keepdims=False)
    for by in (4, 3, 5, 2, 6, 1, 7):
        piece = lax.dynamic_index_in_dim(rows, (z + by) % 8, 0, keepdims=False)
        total = total + shift(piece.astype(BF16), "z", by).astype(F32)
    mine = total.astype(BF16)
    theirs = shift(mine, "yhi", 1)
    first = jnp.where(yhi == 0, mine, theirs)
    second = jnp.where(yhi == 0, theirs, mine)
    ring = ring_of_eight(jnp.concatenate([first, second], axis=1), 32)
    stack = roll_blocks(jnp.stack(ring), (8 - z) % 8, 0).reshape(448, 1024)
    across = shift(stack, "core", 1)
    stack = jnp.stack([stack, across])
    rotated = roll_blocks(stack, core, 0).reshape(896, 1024)
    train_eigen = rotated[768:]
    act = rotated[:768].reshape(2, 8, 2, 2, 12, 1024)
    act = roll_blocks(act, z, 1)
    act = roll_blocks(act, yhi, 2)
    act = roll_blocks(act, core, 3)
    act = act.transpose(0, 3, 2, 1, 4, 5).reshape(2, 4, 2, 48, 1024)
    act = roll_blocks(act, x, 1)
    act = roll_blocks(act, ylo, 2)
    act = act.transpose(0, 2, 1, 3, 4).reshape(2, 384, 1024)

    near = jnp.dot(half_grads, basis_out, preferred_element_type=F32)
    far = jnp.dot(other_grads, basis_out, preferred_element_type=F32)
    pieces = jnp.concatenate([near, far], axis=0).reshape(8, 96, 896)
    grad = scatter_tok(pieces, x, ylo).astype(BF16)
    planes = gather_tok(grad)
    grad = jnp.stack([b for plane in planes for b in plane])
    grad = grad.reshape(8, 4, 2, 12, 896).transpose(2, 0, 1, 3, 4).reshape(2, 384, 896)

    gram = jnp.einsum("qte,qtd->qed", grad, act, preferred_element_type=F32)
    precond = gram * (1.0 / 384) / eigen_grid
    probe = jnp.einsum(
        "qed,kd->eqk", precond.astype(BF16), train_eigen, preferred_element_type=F32
    ).reshape(8, 112, 256)
    probe = scatter_tok(probe, x, ylo).astype(BF16)
    planes = gather_tok(probe)
    probe = jnp.stack([b for plane in planes for b in plane]).reshape(2, 4, 112, 256)
    probe = roll_blocks(probe, (4 - x) % 4, 1)
    probe = roll_blocks(probe, ylo, 0)
    probe = probe.transpose(1, 0, 2, 3).reshape(896, 256)

    pulled = jnp.dot(basis_out, probe, preferred_element_type=F32)
    by_core = pulled.reshape(16, 2, 112, 256)
    keep = lax.dynamic_index_in_dim(by_core, core, 1, keepdims=False)
    give = lax.dynamic_index_in_dim(by_core, 1 - core, 1, keepdims=False)
    chip_sum = keep + shift(give, "core", 1)
    parts = lax.all_to_all(chip_sum.astype(BF16), ("z", "yhi"), 0, 0)
    result = parts.astype(F32).sum(axis=0)
    return result.astype(BF16).reshape(112, 2, 128)


def solution(mesh):
    grid = Mesh(mesh.devices.reshape(tuple(SIZES.values())), tuple(SIZES))
    placed = (
        P(None, None, FEAT),
        P(None, FEAT, TOK),
        P(None, FEAT),
        P(FEAT, TOK),
        P(TOK, FEAT),
        P(FEAT, TOK),
    )
    return jax.shard_map(
        per_device,
        mesh=grid,
        in_specs=placed,
        out_specs=P(TOK + FEAT, None, None),
        check_vma=False,
    )
```

```python
import jax
import jax.numpy as jnp
from jax import lax
from jax.sharding import Mesh, PartitionSpec as P

BF16 = jnp.bfloat16
F32 = jnp.float32
SIZES = {"x": 4, "ylo": 2, "z": 8, "yhi": 2, "core": 2}
TOK = ("x", "ylo")
FEAT = ("z", "yhi", "core")


def swap(array, axis):
    return lax.ppermute(array, axis, [(0, 1), (1, 0)])


def pick(array, index, axis=0):
    return lax.dynamic_index_in_dim(array, index, axis, keepdims=False)


def exchange(pieces, axes):
    return lax.all_to_all(pieces, axes, 0, 0)


def scatter_sum(pieces, axes):
    return exchange(pieces.astype(BF16), axes).astype(F32).sum(axis=0)


def gather(block, axes, count):
    return exchange(jnp.broadcast_to(block[None], (count,) + block.shape), axes)


def direct_gather(own):
    blocks = {(0, 0): own}
    for i, j in ((2, 1), (2, 0), (1, 1), (3, 1), (1, 0), (3, 0), (0, 1)):
        pairs = [
            ((a + i) % 4 * 2 + (b + j) % 2, a * 2 + b) for a in range(4) for b in range(2)
        ]
        blocks[i, j] = lax.ppermute(own, TOK, pairs)
    return jnp.stack([blocks[i, j] for i in range(4) for j in range(2)])


def roll_blocks(array, by):
    twice = jnp.concatenate([array, array], axis=0)
    return lax.dynamic_slice_in_dim(twice, by, array.shape[0], 0)


def in_order(own, index, axis):
    other = swap(own, axis)
    return jnp.where(index == 0, own, other), jnp.where(index == 0, other, own)


def per_device(query_acts, query_grads, train_acts, basis_in, basis_out, eigen_grid):
    x, ylo, yhi, core = (lax.axis_index(a) for a in ("x", "ylo", "yhi", "core"))

    acts = query_acts.reshape(2, 8, 2, 2, 12, 256).transpose(3, 1, 2, 0, 4, 5)
    acts = jnp.concatenate(
        [acts.reshape(2, 8, 48, 256), train_acts.reshape(2, 8, 8, 256)], axis=2
    ).reshape(2, 448, 256)
    give_acts, keep_acts = pick(acts, 1 - core), pick(acts, core)
    give_cols = lax.dynamic_slice_in_dim(basis_in, (1 - yhi) * 512, 512, 1)
    keep_cols = lax.dynamic_slice_in_dim(basis_in, yhi * 512, 512, 1)
    dot = lambda a, b: jnp.dot(a, b, preferred_element_type=F32)

    give, keep = dot(give_acts, give_cols), dot(give_acts, keep_cols)

    own = query_grads.reshape(24, 3584)
    both = in_order(own, yhi, "yhi")
    both, give, keep = lax.optimization_barrier((both, give, keep))
    near_grads = lax.all_gather(jnp.concatenate(both), "z", axis=0, tiled=True)

    give = swap(give, "core") + dot(keep_acts, give_cols)
    keep = swap(keep, "core") + dot(keep_acts, keep_cols)
    pair = keep + swap(give.astype(BF16), "yhi").astype(F32)
    rows = basis_out.reshape(16, 2, 112, 896)
    give_rows = pick(rows, 1 - core, 1).reshape(1792, 896)
    keep_rows = pick(rows, core, 1).reshape(1792, 896)
    pair, give_rows, keep_rows = lax.optimization_barrier((pair, give_rows, keep_rows))
    mine = scatter_sum(pair.reshape(8, 56, 512), "z").astype(BF16)
    mine = jnp.concatenate(in_order(mine, yhi, "yhi"), axis=1)
    near_grads, mine = lax.optimization_barrier((near_grads, mine))
    mine = jnp.concatenate([mine, jnp.zeros((40, 1024), BF16)], axis=0)
    near_rotated = lax.all_gather(mine, "z", axis=0)

    far_grads = swap(near_grads, "core")
    near = dot(near_grads, basis_out).astype(BF16)
    far = dot(far_grads, basis_out).astype(BF16)
    pieces = jnp.concatenate([near, far], axis=0)
    summed = scatter_sum(pieces.reshape(8, 96, 896), TOK).astype(BF16)
    grad = direct_gather(summed)
    near_rotated, _ = lax.optimization_barrier((near_rotated, summed))
    near_rotated = near_rotated[:, :56].reshape(448, 1024)

    rotated = jnp.concatenate([near_rotated, swap(near_rotated, "core")], axis=0)
    train = rotated.reshape(2, 8, 56, 1024)[:, :, 48:].reshape(2, 64, 1024)
    train = jnp.where(core == 0, train, train[::-1]).reshape(128, 1024)
    rotated = rotated.reshape(4, 2, 112, 1024)
    rotated = jnp.where(ylo == 0, rotated, rotated[:, ::-1])
    rotated = roll_blocks(rotated, x).reshape(896, 1024)
    grad, rotated, train = lax.optimization_barrier((grad, rotated, train))
    grad = jnp.pad(grad.reshape(16, 48, 896), ((0, 0), (0, 8), (0, 0)))
    row = jnp.arange(56)
    of_query = (row // 12 % 2)[None, :] == jnp.arange(2)[:, None]
    grad = jnp.where(of_query[:, None, :, None], grad[None], 0).reshape(2, 896, 896)

    gram = jnp.einsum("qte,td->qed", grad, rotated, preferred_element_type=F32)
    precond = gram * (1.0 / 384) / eigen_grid
    probe = jnp.einsum(
        "qed,kd->eqk", precond.astype(BF16), train, preferred_element_type=F32
    )
    probe = scatter_sum(probe.reshape(8, 112, 256), TOK).astype(BF16)
    probe = gather(probe, TOK, 8).reshape(896, 256)

    chip = swap(dot(give_rows, probe).astype(BF16), "core").astype(F32)
    chip = (dot(keep_rows, probe) + chip).reshape(16, 112, 256)
    pulled = scatter_sum(chip, ("z", "yhi"))
    return pulled.astype(BF16).reshape(112, 2, 128)


def solution(mesh):
    grid = Mesh(mesh.devices.reshape(tuple(SIZES.values())), tuple(SIZES))
    placed = (
        P(None, None, FEAT),
        P(None, FEAT, TOK),
        P(None, FEAT),
        P(FEAT, TOK),
        P(TOK, FEAT),
        P(FEAT, TOK),
    )
    return jax.shard_map(
        per_device,
        mesh=grid,
        in_specs=placed,
        out_specs=P(TOK + FEAT, None, None),
        check_vma=False,
    )
```

```python
import jax
import jax.numpy as jnp
from jax import lax
from jax.sharding import Mesh, PartitionSpec as P

BF16 = jnp.bfloat16
F32 = jnp.float32
SIZES = {"x": 4, "ylo": 2, "z": 8, "yhi": 2, "core": 2}
TOK = ("x", "ylo")
FEAT = ("z", "yhi", "core")


def swap(array, axis):
    return lax.ppermute(array, axis, [(0, 1), (1, 0)])


def pick(array, index, axis=0):
    return lax.dynamic_index_in_dim(array, index, axis, keepdims=False)


def exchange(pieces, axes):
    return lax.all_to_all(pieces, axes, 0, 0)


def scatter_sum(pieces, axes):
    return exchange(pieces.astype(BF16), axes).astype(F32).sum(axis=0)


def gather(block, axes, count):
    return exchange(jnp.broadcast_to(block[None], (count,) + block.shape), axes)


def direct_gather(own):
    blocks = {(0, 0): own}
    for i, j in ((2, 1), (2, 0), (1, 1), (3, 1), (1, 0), (3, 0), (0, 1)):
        pairs = [
            ((a + i) % 4 * 2 + (b + j) % 2, a * 2 + b) for a in range(4) for b in range(2)
        ]
        blocks[i, j] = lax.ppermute(own, TOK, pairs)
    return jnp.stack([blocks[i, j] for i in range(4) for j in range(2)])


def roll_blocks(array, by):
    twice = jnp.concatenate([array, array], axis=0)
    return lax.dynamic_slice_in_dim(twice, by, array.shape[0], 0)


def shift(array, by):
    return lax.ppermute(array, "z", [(i, (i + by) % 8) for i in range(8)])


def place(blocks, block, at):
    return lax.dynamic_update_slice(blocks, block[None], (at % 8, 0, 0))


def ring_of_eight(own, z, beside):
    forward = backward = own
    blocks = place(jnp.zeros((8,) + own.shape, own.dtype), own, z)
    done = {}
    for hop in (1, 2, 3):
        forward, backward = shift(forward, 1), shift(backward, -1)
        if hop in beside:
            forward, backward, done[hop] = lax.optimization_barrier(
                (forward, backward, beside[hop](done))
            )
        blocks = place(place(blocks, forward, z - hop + 8), backward, z + hop)
    half = own.shape[0] // 2
    far = [shift(forward[:half], 1), shift(backward[half:], -1)]
    return place(blocks, jnp.concatenate(far, axis=0), z + 4), done


def direct_gather_z(own, z):
    blocks = {0: own} | {k: shift(own, -k) for k in (4, 3, 5, 2, 6, 1, 7)}
    return roll_blocks(jnp.stack([blocks[k] for k in range(8)]), (8 - z) % 8)


def in_order(own, index, axis):
    other = swap(own, axis)
    return jnp.where(index == 0, own, other), jnp.where(index == 0, other, own)


def per_device(query_acts, query_grads, train_acts, basis_in, basis_out, eigen_grid):
    x, ylo, z, yhi, core = (lax.axis_index(a) for a in SIZES)

    acts = query_acts.reshape(2, 8, 2, 2, 12, 256).transpose(3, 1, 2, 0, 4, 5)
    acts = jnp.concatenate(
        [acts.reshape(2, 8, 48, 256), train_acts.reshape(2, 8, 8, 256)], axis=2
    ).reshape(2, 448, 256)
    give_acts, keep_acts = pick(acts, 1 - core), pick(acts, core)
    give_cols = lax.dynamic_slice_in_dim(basis_in, (1 - yhi) * 512, 512, 1)
    keep_cols = lax.dynamic_slice_in_dim(basis_in, yhi * 512, 512, 1)
    dot = lambda a, b: jnp.dot(a, b, preferred_element_type=F32)

    give, keep = dot(give_acts, give_cols), dot(give_acts, keep_cols)

    def chip_sums(done):
        first = swap(give, "core") + dot(keep_acts, give_cols)
        second = swap(keep, "core") + dot(keep_acts, keep_cols)
        return first.astype(BF16), second, basis_out.reshape(16, 2, 112, 896)

    def pair_sums(done):
        first, second, rows = done[1]
        give_rows = pick(rows, 1 - core, 1).reshape(1792, 896)
        keep_rows = pick(rows, core, 1).reshape(1792, 896)
        return second + swap(first, "yhi").astype(F32), give_rows, keep_rows

    own = query_grads.reshape(24, 3584)
    both = in_order(own, yhi, "yhi")
    both, give, keep = lax.optimization_barrier((both, give, keep))
    near_grads, done = ring_of_eight(
        jnp.concatenate(both), z, {1: chip_sums, 3: pair_sums}
    )
    near_grads = near_grads.reshape(384, 3584)
    pair, give_rows, keep_rows = done[3]
    arrived = exchange(pair.reshape(8, 56, 512).astype(BF16), "z")

    far_grads = swap(near_grads, "core")
    near = dot(near_grads, basis_out).astype(BF16)
    far = dot(far_grads, basis_out).astype(BF16)
    pieces = jnp.concatenate([near, far], axis=0)
    pieces, arrived = lax.optimization_barrier((pieces, arrived))
    mine = arrived.astype(F32).sum(axis=0).astype(BF16)
    mine = jnp.concatenate(in_order(mine, yhi, "yhi"), axis=1)
    near_rotated = direct_gather_z(mine, z).reshape(448, 1024)
    summed = scatter_sum(pieces.reshape(8, 96, 896), TOK).astype(BF16)
    grad = direct_gather(summed)
    near_rotated, _ = lax.optimization_barrier((near_rotated, summed))

    rotated = jnp.concatenate([near_rotated, swap(near_rotated, "core")], axis=0)
    train = rotated.reshape(2, 8, 56, 1024)[:, :, 48:].reshape(2, 64, 1024)
    train = jnp.where(core == 0, train, train[::-1]).reshape(128, 1024)
    rotated = rotated.reshape(4, 2, 112, 1024)
    rotated = jnp.where(ylo == 0, rotated, rotated[:, ::-1])
    rotated = roll_blocks(rotated, x).reshape(896, 1024)
    grad, rotated, train = lax.optimization_barrier((grad, rotated, train))
    grad = jnp.pad(grad.reshape(16, 48, 896), ((0, 0), (0, 8), (0, 0)))
    row = jnp.arange(56)
    of_query = (row // 12 % 2)[None, :] == jnp.arange(2)[:, None]
    grad = jnp.where(of_query[:, None, :, None], grad[None], 0).reshape(2, 896, 896)

    gram = jnp.einsum("qte,td->qed", grad, rotated, preferred_element_type=F32)
    precond = gram * (1.0 / 384) / eigen_grid
    probe = jnp.einsum(
        "qed,kd->eqk", precond.astype(BF16), train, preferred_element_type=F32
    )
    probe = scatter_sum(probe.reshape(8, 112, 256), TOK).astype(BF16)
    probe = gather(probe, TOK, 8).reshape(896, 256)

    chip = swap(dot(give_rows, probe).astype(BF16), "core").astype(F32)
    chip = (dot(keep_rows, probe) + chip).reshape(16, 112, 256)
    pulled = scatter_sum(chip, ("z", "yhi"))
    return pulled.astype(BF16).reshape(112, 2, 128)


def solution(mesh):
    grid = Mesh(mesh.devices.reshape(tuple(SIZES.values())), tuple(SIZES))
    placed = (
        P(None, None, FEAT),
        P(None, FEAT, TOK),
        P(None, FEAT),
        P(FEAT, TOK),
        P(TOK, FEAT),
        P(FEAT, TOK),
    )
    return jax.shard_map(
        per_device,
        mesh=grid,
        in_specs=placed,
        out_specs=P(TOK + FEAT, None, None),
        check_vma=False,
    )
```

```python
import jax
import jax.numpy as jnp
from jax import lax
from jax.sharding import Mesh, PartitionSpec as P

BF16 = jnp.bfloat16
F32 = jnp.float32
SIZES = {"x": 4, "ylo": 2, "z": 8, "yhi": 2, "core": 2}
TOK = ("x", "ylo")
FEAT = ("z", "yhi", "core")


def swap(array, axis):
    return lax.ppermute(array, axis, [(0, 1), (1, 0)])


def pick(array, index, axis=0):
    return lax.dynamic_index_in_dim(array, index, axis, keepdims=False)


def exchange(pieces, axes):
    return lax.all_to_all(pieces, axes, 0, 0)


def scatter_sum(pieces, axes):
    return exchange(pieces.astype(BF16), axes).astype(F32).sum(axis=0)


def gather(block, axes, count):
    return exchange(jnp.broadcast_to(block[None], (count,) + block.shape), axes)


def direct_gather(own):
    blocks = {(0, 0): own}
    for i, j in ((2, 1), (2, 0), (1, 1), (3, 1), (1, 0), (3, 0), (0, 1)):
        pairs = [
            ((a + i) % 4 * 2 + (b + j) % 2, a * 2 + b) for a in range(4) for b in range(2)
        ]
        blocks[i, j] = lax.ppermute(own, TOK, pairs)
    return jnp.stack([blocks[i, j] for i in range(4) for j in range(2)])


def roll_blocks(array, by):
    twice = jnp.concatenate([array, array], axis=0)
    return lax.dynamic_slice_in_dim(twice, by, array.shape[0], 0)


def in_order(own, index, axis):
    other = swap(own, axis)
    return jnp.where(index == 0, own, other), jnp.where(index == 0, other, own)


def per_device(query_acts, query_grads, train_acts, basis_in, basis_out, eigen_grid):
    x, ylo, yhi, core = (lax.axis_index(a) for a in ("x", "ylo", "yhi", "core"))

    acts = query_acts.reshape(2, 8, 2, 2, 12, 256).transpose(3, 1, 2, 0, 4, 5)
    acts = jnp.concatenate(
        [acts.reshape(2, 8, 48, 256), train_acts.reshape(2, 8, 8, 256)], axis=2
    ).reshape(2, 448, 256)
    give_acts, keep_acts = pick(acts, 1 - core), pick(acts, core)
    give_cols = lax.dynamic_slice_in_dim(basis_in, (1 - yhi) * 512, 512, 1)
    keep_cols = lax.dynamic_slice_in_dim(basis_in, yhi * 512, 512, 1)
    dot = lambda a, b: jnp.dot(a, b, preferred_element_type=F32)

    give, keep = dot(give_acts, give_cols), dot(give_acts, keep_cols)

    own = query_grads.reshape(24, 3584)
    both = in_order(own, yhi, "yhi")
    both, give, keep = lax.optimization_barrier((both, give, keep))
    near_grads = lax.all_gather(jnp.concatenate(both), "z", axis=0, tiled=True)

    give = swap(give, "core") + dot(keep_acts, give_cols)
    keep = swap(keep, "core") + dot(keep_acts, keep_cols)
    pair = keep + swap(give.astype(BF16), "yhi").astype(F32)
    rows = basis_out.reshape(16, 2, 112, 896)
    give_rows = pick(rows, 1 - core, 1).reshape(1792, 896)
    keep_rows = pick(rows, core, 1).reshape(1792, 896)
    pair, give_rows, keep_rows = lax.optimization_barrier((pair, give_rows, keep_rows))
    mine = scatter_sum(pair.reshape(8, 56, 512), "z").astype(BF16)
    mine = jnp.concatenate(in_order(mine, yhi, "yhi"), axis=1)
    near_grads, mine = lax.optimization_barrier((near_grads, mine))
    mine = jnp.concatenate([mine, jnp.zeros((40, 1024), BF16)], axis=0)
    near_rotated = lax.all_gather(mine, "z", axis=0)

    far_grads = swap(near_grads, "core")
    near = dot(near_grads, basis_out).astype(BF16).reshape(8, 48, 896)
    far = dot(far_grads, basis_out).astype(BF16).reshape(8, 48, 896)
    pieces = jnp.stack([near, far], axis=1).reshape(8, 96, 896)
    summed = scatter_sum(pieces, TOK).astype(BF16)
    grad = direct_gather(summed)

    near_rotated, _ = lax.optimization_barrier((near_rotated, summed))
    near_rotated = near_rotated[:, :56].reshape(4, 2, 56, 1024)
    near_rotated = jnp.where(ylo == 0, near_rotated, near_rotated[:, ::-1])
    near_rotated = roll_blocks(near_rotated, x).reshape(448, 1024)
    rotated = jnp.concatenate([near_rotated, swap(near_rotated, "core")], axis=0)
    train = rotated.reshape(2, 4, 2, 56, 1024)[:, :, :, 48:]
    train = jnp.where(core == 0, train, train[::-1])
    train = jnp.where(ylo == 0, train, train[:, :, ::-1])
    train = roll_blocks(train.swapaxes(0, 1), (4 - x) % 4).swapaxes(0, 1)
    train = train.reshape(128, 1024)
    grad, rotated, train = lax.optimization_barrier((grad, rotated, train))
    grad = grad.reshape(8, 2, 48, 896).swapaxes(0, 1).reshape(16, 48, 896)
    grad = jnp.pad(grad, ((0, 0), (0, 8), (0, 0)))
    row = jnp.arange(56)
    of_query = (row // 12 % 2)[None, :] == jnp.arange(2)[:, None]
    grad = jnp.where(of_query[:, None, :, None], grad[None], 0).reshape(2, 896, 896)

    gram = jnp.einsum("qte,td->qed", grad, rotated, preferred_element_type=F32)
    precond = gram * (1.0 / 384) / eigen_grid
    probe = jnp.einsum(
        "qed,kd->eqk", precond.astype(BF16), train, preferred_element_type=F32
    )
    probe = scatter_sum(probe.reshape(8, 112, 256), TOK).astype(BF16)
    probe = gather(probe, TOK, 8).reshape(896, 256)

    chip = swap(dot(give_rows, probe).astype(BF16), "core").astype(F32)
    chip = (dot(keep_rows, probe) + chip).reshape(16, 112, 256)
    pulled = scatter_sum(chip, ("z", "yhi"))
    return pulled.astype(BF16).reshape(112, 2, 128)


def solution(mesh):
    grid = Mesh(mesh.devices.reshape(tuple(SIZES.values())), tuple(SIZES))
    placed = (
        P(None, None, FEAT),
        P(None, FEAT, TOK),
        P(None, FEAT),
        P(FEAT, TOK),
        P(TOK, FEAT),
        P(FEAT, TOK),
    )
    return jax.shard_map(
        per_device,
        mesh=grid,
        in_specs=placed,
        out_specs=P(TOK + FEAT, None, None),
        check_vma=False,
    )
```

```python
import jax
import jax.numpy as jnp
from jax import lax
from jax.sharding import Mesh, PartitionSpec as P

BF16 = jnp.bfloat16
F32 = jnp.float32
SIZES = {"x": 4, "ylo": 2, "z": 8, "yhi": 2, "core": 2}
TOK = ("x", "ylo")
FEAT = ("z", "yhi", "core")


def swap(array, axis):
    return lax.ppermute(array, axis, [(0, 1), (1, 0)])


def pick(array, index, axis=0):
    return lax.dynamic_index_in_dim(array, index, axis, keepdims=False)


def exchange(pieces, axes):
    return lax.all_to_all(pieces, axes, 0, 0)


def scatter_sum(pieces, axes):
    return exchange(pieces.astype(BF16), axes).astype(F32).sum(axis=0)


def gather(block, axes, count):
    return exchange(jnp.broadcast_to(block[None], (count,) + block.shape), axes)


def direct_gather(own):
    blocks = {(0, 0): own}
    for i, j in ((2, 1), (1, 1), (3, 1), (0, 1), (2, 0), (1, 0), (3, 0)):
        pairs = [
            ((a + i) % 4 * 2 + (b + j) % 2, a * 2 + b) for a in range(4) for b in range(2)
        ]
        blocks[i, j] = lax.ppermute(own, TOK, pairs)
    return jnp.stack([blocks[i, j] for i in range(4) for j in range(2)])


def roll_blocks(array, by):
    twice = jnp.concatenate([array, array], axis=0)
    return lax.dynamic_slice_in_dim(twice, by, array.shape[0], 0)


def in_order(own, index, axis):
    other = swap(own, axis)
    return jnp.where(index == 0, own, other), jnp.where(index == 0, other, own)


def per_device(query_acts, query_grads, train_acts, basis_in, basis_out, eigen_grid):
    x, ylo, yhi, core = (lax.axis_index(a) for a in ("x", "ylo", "yhi", "core"))

    acts = query_acts.reshape(2, 8, 2, 2, 12, 256).transpose(3, 1, 2, 0, 4, 5)
    acts = jnp.concatenate(
        [acts.reshape(2, 8, 48, 256), train_acts.reshape(2, 8, 8, 256)], axis=2
    ).reshape(2, 448, 256)
    give_acts, keep_acts = pick(acts, 1 - core), pick(acts, core)
    give_cols = lax.dynamic_slice_in_dim(basis_in, (1 - yhi) * 512, 512, 1)
    keep_cols = lax.dynamic_slice_in_dim(basis_in, yhi * 512, 512, 1)
    dot = lambda a, b: jnp.dot(a, b, preferred_element_type=F32)

    give, keep = dot(give_acts, give_cols), dot(give_acts, keep_cols)

    own = query_grads.reshape(24, 3584)
    both = in_order(own, yhi, "yhi")
    both, give, keep = lax.optimization_barrier((both, give, keep))
    near_grads = lax.all_gather(jnp.concatenate(both), "z", axis=0, tiled=True)

    give = swap(give, "core") + dot(keep_acts, give_cols)
    keep = swap(keep, "core") + dot(keep_acts, keep_cols)
    pair = keep + swap(give.astype(BF16), "yhi").astype(F32)
    rows = basis_out.reshape(16, 2, 112, 896)
    give_rows = pick(rows, 1 - core, 1).reshape(1792, 896)
    keep_rows = pick(rows, core, 1).reshape(1792, 896)
    pair, give_rows, keep_rows = lax.optimization_barrier((pair, give_rows, keep_rows))
    mine = scatter_sum(pair.reshape(8, 56, 512), "z").astype(BF16)
    mine = jnp.concatenate(in_order(mine, yhi, "yhi"), axis=1)
    near_grads, mine = lax.optimization_barrier((near_grads, mine))
    mine = jnp.concatenate([mine, jnp.zeros((40, 1024), BF16)], axis=0)
    near_rotated = lax.all_gather(mine, "z", axis=0)

    far_grads = swap(near_grads, "core")
    near = dot(near_grads, basis_out).astype(BF16).reshape(8, 48, 896)
    far = dot(far_grads, basis_out).astype(BF16).reshape(8, 48, 896)
    pieces = jnp.stack([near, far], axis=1).reshape(8, 96, 896)
    summed = scatter_sum(pieces, TOK).astype(BF16)
    grad = direct_gather(summed)

    near_rotated, _ = lax.optimization_barrier((near_rotated, summed))
    near_rotated = near_rotated[:, :56].reshape(4, 2, 56, 1024)
    near_rotated = jnp.where(ylo == 0, near_rotated, near_rotated[:, ::-1])
    near_rotated = roll_blocks(near_rotated, x).reshape(448, 1024)
    rotated = jnp.concatenate([near_rotated, swap(near_rotated, "core")], axis=0)
    train = rotated.reshape(2, 4, 2, 56, 1024)[:, :, :, 48:]
    train = jnp.where(core == 0, train, train[::-1])
    train = jnp.where(ylo == 0, train, train[:, :, ::-1])
    train = roll_blocks(train.swapaxes(0, 1), (4 - x) % 4).swapaxes(0, 1)
    train = train.reshape(128, 1024)
    grad, rotated, train = lax.optimization_barrier((grad, rotated, train))
    grad = grad.reshape(8, 2, 48, 896).swapaxes(0, 1).reshape(16, 48, 896)
    grad = jnp.pad(grad, ((0, 0), (0, 8), (0, 0)))
    row = jnp.arange(56)
    of_query = (row // 12 % 2)[None, :] == jnp.arange(2)[:, None]
    grad = jnp.where(of_query[:, None, :, None], grad[None], 0).reshape(2, 896, 896)

    gram = jnp.einsum("qte,td->qed", grad, rotated, preferred_element_type=F32)
    precond = gram * (1.0 / 384) / eigen_grid
    probe = jnp.einsum(
        "qed,kd->eqk", precond.astype(BF16), train, preferred_element_type=F32
    )
    probe = scatter_sum(probe.reshape(8, 112, 256), TOK).astype(BF16)
    probe = gather(probe, TOK, 8).reshape(896, 256)

    chip = swap(dot(give_rows, probe).astype(BF16), "core").astype(F32)
    chip = (dot(keep_rows, probe) + chip).reshape(16, 112, 256)
    pulled = scatter_sum(chip, ("z", "yhi"))
    return pulled.astype(BF16).reshape(112, 2, 128)


def solution(mesh):
    grid = Mesh(mesh.devices.reshape(tuple(SIZES.values())), tuple(SIZES))
    placed = (
        P(None, None, FEAT),
        P(None, FEAT, TOK),
        P(None, FEAT),
        P(FEAT, TOK),
        P(TOK, FEAT),
        P(FEAT, TOK),
    )
    return jax.shard_map(
        per_device,
        mesh=grid,
        in_specs=placed,
        out_specs=P(TOK + FEAT, None, None),
        check_vma=False,
    )
```
